32 devices in a mesh: groups: 2 (over x), op: 16 (over z, y, core).
Axes of the slice: x: 2, y: 2, z: 4, core: 2. Of those that a mesh axis runs over, the one named last changes fastest.
Arguments:
- psi: bfloat16 [32, 256, 256], P(('groups', 'op')), parts along dimension 0, may hold values from -60 to 60
- left_ops: bfloat16 [256, 256, 256], P(('groups', 'op')), parts along dimension 0, may hold values from -0.375 to 0.375
- right_ops: bfloat16 [256, 256, 256], P(('groups', 'op')), parts along dimension 0, may hold values from -0.03125 to 0.03125
- pair_term: int32 [2048], P('op'), may hold values from 0 to 127, as said below
- pair_source: int32 [2048], P('op'), may hold values from 0 to 15, as said below
- pair_target: int32 [2048], P('op'), may hold values from 0 to 15, as said below
- right_order: int32 [16], replicated, may hold values from 0 to 15, as said below
Outputs:
- sigma_one: bfloat16 [32, 256, 256], P(('groups', 'op')), parts along dimension 0
- sigma_two: bfloat16 [32, 256, 256], P(('groups', 'op')), parts along dimension 0
The draws below stay inside these ranges and needn't reach their ends.
There are 2 independent parts, one for each index of `groups`. The reference program is written for one: setup_inputs(seed, part) draws one part's arguments, and reference() takes and returns one part's arrays. A program takes and returns all parts, laid end to end along the dimension named above; an argument that names none is the same for every part. Nothing has to cross between parts.
Inputs may be any that keep to these rules, and one draw needn't show every extreme that they name: `pair_term`: pair p names a term of the same device's block: from (p // 128) * 8 to that plus 8 - 1. `pair_source`: every sector is read by exactly 128 pairs. `pair_target`: every sector receives exactly 128 pairs; with M = 16, the pairs of block d (pairs d * 128 to d * 128 + 127) add only to sectors whose position j in right_order satisfies j // 1 in d, d + 1, d - 1, d + M // 2, counted modulo M, and 32 of them to each of these four. `right_order`: each sector number appears once.
All inputs are finite; a program needn't handle non-finite values.
Results may differ from the reference program's by a relative error of at most 0.0062.
Values may be sent and summed in bfloat16 or wider, within the bound.
No kernel may reach another device: no remote copies, remote signals or barrier semaphores. Data moves between devices by JAX's collectives and lax.ppermute only.
A program may use at most 192 MiB of HBM per device.

```python
import jax
import jax.numpy as jnp
from jax import lax

SB = 256
SEC_DEV = 1
TERM_DEV = 8
BAND = 4
PAIRS_DEV = 128
SECTORS = 16
TERMS = 128
PAIRS = 2048


def shared_order(key):
    return jax.random.permutation(jax.random.fold_in(key, 7), SECTORS).astype(jnp.int32)


def draw_psi(key, part):
    key = jax.random.fold_in(key, 21)
    ranks = jax.random.permutation(jax.random.fold_in(key, 1), SECTORS).astype(jnp.float32)
    scales = jnp.exp(jnp.log(10.0) * ranks / (SECTORS - 1))
    entries = jnp.clip(jax.random.normal(jax.random.fold_in(key, 2), (SECTORS, SB, SB), jnp.float32), -6.0, 6.0)
    return (entries * scales[:, None, None]).astype(jnp.bfloat16)


def draw_pair_term(key, part):
    key = jax.random.fold_in(key, 11)
    local_term = jax.random.randint(key, (PAIRS,), 0, TERM_DEV)
    block = jnp.arange(PAIRS, dtype=jnp.int32) // PAIRS_DEV
    return (block * TERM_DEV + local_term).astype(jnp.int32)


def draw_pair_source(key, part):
    key = jax.random.fold_in(key, 12)
    return (jax.random.permutation(key, PAIRS) % SECTORS).astype(jnp.int32)


def draw_pair_target(key, part):
    order = shared_order(key)
    key = jax.random.fold_in(key, 13)
    blocks = PAIRS // PAIRS_DEV
    keys = jax.random.split(key, blocks)
    choice_index = jax.vmap(lambda one: jax.random.permutation(one, PAIRS_DEV) % BAND)(keys)
    reach_table = jnp.array([0, 1, blocks - 1, blocks // 2], dtype=jnp.int32)
    offsets = jnp.take(reach_table, choice_index.astype(jnp.int32))
    within = jax.random.randint(jax.random.fold_in(key, 5), (blocks, PAIRS_DEV), 0, SEC_DEV)
    device = jnp.arange(blocks, dtype=jnp.int32)[:, None]
    owner = (device + offsets) % blocks
    position = (owner * SEC_DEV + within).reshape(PAIRS).astype(jnp.int32)
    return jnp.take(order, position).astype(jnp.int32)


def draw_right_order(key, part):
    return shared_order(key)


def level_of(own_key, extent, shards, low, top_value):
    def one(dim, blocks):
        draws = jax.random.uniform(jax.random.fold_in(jax.random.fold_in(own_key, 6), dim), (blocks,), jnp.float32, low / len(shards), top_value / len(shards))
        return jnp.repeat(jnp.exp(draws), extent[dim] // blocks).reshape((-1,) + (1,) * (len(extent) - dim - 1))

    factor_of = one(*shards[0])
    for cut in shards[1:]:
        factor_of = factor_of * one(*cut)
    return factor_of


def centred(rng, dims, deviation, bound, pieces=(), held_as=jnp.bfloat16):
    values = deviation * jax.random.normal(rng, dims, jnp.float32)
    if pieces:
        values = values * level_of(rng, dims, pieces, -0.22, 0.18)
    return jnp.clip(values, -bound, bound).astype(held_as)


def setup_inputs(seed: int = 0, part: int = 0) -> dict:
    arg_keys = jax.random.split(jax.random.key(seed), 8)
    own_keys = jax.random.split(jax.random.fold_in(arg_keys[7], part), 8)
    psi = draw_psi(jax.random.fold_in(jax.random.fold_in(arg_keys[7], part), 71), part)
    left_ops = centred(own_keys[1], (TERMS, SB, SB), SB ** -0.5, 0.375, ((0, 16),))
    right_ops = centred(own_keys[2], (TERMS, SB, SB), (SB * PAIRS_DEV // SEC_DEV) ** -0.5, 0.03125, ((0, 16),))
    pair_term = draw_pair_term(jax.random.fold_in(arg_keys[7], 71), part)
    pair_source = draw_pair_source(jax.random.fold_in(arg_keys[7], 71), part)
    pair_target = draw_pair_target(jax.random.fold_in(arg_keys[7], 71), part)
    right_order = draw_right_order(jax.random.fold_in(arg_keys[7], 71), part)
    return {"psi": psi, "left_ops": left_ops, "right_ops": right_ops, "pair_term": pair_term, "pair_source": pair_source, "pair_target": pair_target, "right_order": right_order}


def apply_ham(field, left_ops, right_ops, pair_term, pair_source, pair_target):

    def step(index, total):
        term_idx = pair_term[index]
        half = jnp.dot(left_ops[term_idx], field[pair_source[index]], preferred_element_type=jnp.float32).astype(jnp.bfloat16)
        piece = jnp.dot(half, right_ops[term_idx], preferred_element_type=jnp.float32)
        return total.at[pair_target[index]].add(piece)
    start = jnp.zeros((SECTORS, SB, SB), jnp.float32)
    return lax.fori_loop(0, PAIRS, step, start)

def reference(psi, left_ops, right_ops, pair_term, pair_source, pair_target, right_order):
    raw = apply_ham(psi, left_ops, right_ops, pair_term, pair_source, pair_target)
    wave = psi.astype(jnp.float32)
    numer = jnp.sum(wave * raw)
    denom = jnp.sum(wave * wave)
    theta = numer / denom
    rms = jnp.sqrt(denom / (SECTORS * SB * SB))
    first = raw / rms
    resid = ((raw - theta * wave) / rms).astype(jnp.bfloat16)
    second = apply_ham(resid, left_ops, right_ops, pair_term, pair_source, pair_target)
    return (first[right_order].astype(jnp.bfloat16), second[right_order].astype(jnp.bfloat16))
```

```python
import functools

import jax
import jax.numpy as jnp
from jax import lax
from jax.experimental import pallas as pl
from jax.experimental.pallas import tpu as pltpu
from jax.sharding import PartitionSpec as P

STRIP = 16
VMEM = pltpu.VMEM


def in_vmem(x):
    return pltpu.with_memory_space_constraint(x, VMEM)


def fold_sum(x):
    return jnp.sum(x.reshape(x.shape[0] // 8, 8, x.shape[1]), axis=0)


def products(count, slots, *refs):
    w_ref, left_ref, right_ref = refs[:3]
    blocks = refs[3 : 3 + count]
    outs = refs[3 + count : 3 + count + slots]
    mixed, inner = refs[-2:]
    terms, size = right_ref.shape[0], right_ref.shape[1]
    for strip in range(size // STRIP):
        rows = slice(strip * STRIP, (strip + 1) * STRIP)
        stacked = jnp.concatenate([block[rows, :] for block in blocks], axis=0)
        value = jnp.dot(w_ref[...], stacked, preferred_element_type=jnp.float32)
        mixed[:, rows, :] = value.astype(jnp.bfloat16).reshape(terms * slots, STRIP, size)
    for k in range(terms):
        value = jnp.dot(
            mixed[k * slots : (k + 1) * slots].reshape(slots * size, size),
            right_ref[k],
            preferred_element_type=jnp.float32,
        ).astype(jnp.bfloat16)
        for t in range(slots):
            inner[t, k * size : (k + 1) * size, :] = value[t * size : (t + 1) * size]
    for t in range(slots):
        total = jnp.dot(left_ref[...], inner[t], preferred_element_type=jnp.float32)
        outs[t][...] = total.astype(outs[t].dtype)


def partial_sums(weights, left_cat, right_ops, blocks, dtypes):
    count, slots = len(blocks), len(dtypes)
    terms, size = right_ops.shape[0], right_ops.shape[1]
    flops = 2 * size**3 * terms * slots * 3
    return pl.pallas_call(
        functools.partial(products, count, slots),
        out_shape=[jax.ShapeDtypeStruct((size, size), dtype) for dtype in dtypes],
        in_specs=[pl.BlockSpec(memory_space=VMEM)] * (3 + count),
        out_specs=[pl.BlockSpec(memory_space=VMEM)] * slots,
        scratch_shapes=[
            pltpu.VMEM((terms * slots, size, size), jnp.bfloat16),
            pltpu.VMEM((slots, terms * size, size), jnp.bfloat16),
        ],
        cost_estimate=pl.CostEstimate(flops=flops, bytes_accessed=1 << 20, transcendentals=0),
        compiler_params=pltpu.CompilerParams(vmem_limit_bytes=24 << 20),
    )(*[in_vmem(x) for x in (weights, left_cat, right_ops, *blocks)])


def keep_body(count, *refs):
    blocks, stack, squares = refs[:count], refs[count], refs[count + 1]
    total = jnp.zeros(squares.shape, jnp.float32)
    for m in range(count):
        value = blocks[m][...]
        stack[m] = value
        wide = value.astype(jnp.float32)
        total = total + fold_sum(wide * wide)
    squares[...] = total


def keep(blocks):
    count, size = len(blocks), blocks[0].shape[0]
    return pl.pallas_call(
        functools.partial(keep_body, count),
        out_shape=[
            jax.ShapeDtypeStruct((count, size, size), jnp.bfloat16),
            jax.ShapeDtypeStruct((8, size), jnp.float32),
        ],
        in_specs=[pl.BlockSpec(memory_space=VMEM)] * count,
        out_specs=[pl.BlockSpec(memory_space=VMEM)] * 2,
        cost_estimate=pl.CostEstimate(flops=3 << 20, bytes_accessed=4 << 20, transcendentals=0),
        compiler_params=pltpu.CompilerParams(vmem_limit_bytes=16 << 20),
    )(*[in_vmem(x) for x in blocks])


def overlap_body(count, index_ref, stack, *refs):
    blocks, out = refs[:count], refs[count]
    total = jnp.zeros(out.shape, jnp.float32)
    for m in range(count):
        wave = stack[index_ref[m]].astype(jnp.float32)
        total = total + fold_sum(wave * blocks[m][...].astype(jnp.float32))
    out[...] = total


def overlap(index, stack, blocks):
    count, size = len(blocks), blocks[0].shape[0]
    return pl.pallas_call(
        functools.partial(overlap_body, count),
        out_shape=jax.ShapeDtypeStruct((8, size), jnp.float32),
        in_specs=[pl.BlockSpec(memory_space=pltpu.SMEM)] + [pl.BlockSpec(memory_space=VMEM)] * (1 + count),
        out_specs=pl.BlockSpec(memory_space=VMEM),
        cost_estimate=pl.CostEstimate(flops=3 << 20, bytes_accessed=4 << 20, transcendentals=0),
        compiler_params=pltpu.CompilerParams(vmem_limit_bytes=16 << 20),
    )(index, in_vmem(stack), *[in_vmem(x) for x in blocks])


def swap(x, count, mask):
    return lax.ppermute(x, "op", [(i, i ^ mask) for i in range(count)])


def shift(x, count, step):
    return lax.ppermute(x, "op", [(i, (i + step) % count) for i in range(count)])


def gather_blocks(field, count):
    blocks = {0: field}
    if count > 2:
        blocks[2] = swap(field, count, 2)
    for mask in range(4, count, 4):
        blocks[mask] = swap(field, count, mask)
    for mask in range(4, count, 4):
        blocks[mask + 2] = swap(blocks[mask], count, 2)
    for mask in range(0, count, 2):
        blocks[mask + 1] = swap(blocks[mask], count, 1)
    return [blocks[m] for m in range(count)]


def on_device(count, psi, left_ops, right_ops, pair_term, pair_source, pair_target, right_order):
    field = psi[0]
    size = field.shape[0]
    term_rows = left_ops.shape[0]
    me = lax.axis_index("op")
    positions = jnp.arange(count, dtype=jnp.int32)

    def place_of(sector):
        hit = sector[:, None] == right_order[None, :]
        return jnp.sum(jnp.where(hit, positions[None, :], 0), axis=1)

    local_term = pair_term - me * term_rows
    offset = jnp.remainder(place_of(pair_target) - me, count)
    reach = (count // 2, 1, count - 1, 0)

    def weights_of(source, slots):
        source_hit = (jnp.bitwise_xor(source, me)[:, None] == positions[None, :]).astype(jnp.bfloat16)
        wanted = jnp.array([reach[t] for t in slots], jnp.int32)
        combo_hit = (
            (local_term[:, None, None] == jnp.arange(term_rows, dtype=jnp.int32)[None, :, None])
            & (offset[:, None, None] == wanted[None, None, :])
        ).astype(jnp.bfloat16)
        combos = term_rows * len(slots)
        counts = lax.dot_general(
            combo_hit.reshape(-1, combos), source_hit, (((0,), (0,)), ((), ())), preferred_element_type=jnp.float32
        )
        rows = jnp.repeat(jnp.repeat(counts, STRIP, axis=0), STRIP, axis=1)
        same = (jnp.arange(combos * STRIP) % STRIP)[:, None] == (jnp.arange(count * STRIP) % STRIP)[None, :]
        return jnp.where(same, rows, 0.0).astype(jnp.bfloat16)

    left_cat = jnp.transpose(left_ops, (1, 0, 2)).reshape(size, term_rows * size)
    bf16, f32 = jnp.bfloat16, jnp.float32

    def apply_ham(field, source):
        blocks = gather_blocks(field, count)
        (far,) = partial_sums(weights_of(source, (0,)), left_cat, right_ops, blocks, (bf16,))
        far_in = shift(far, count, count // 2)
        up, down, own = partial_sums(weights_of(source, (1, 2, 3)), left_cat, right_ops, blocks, (bf16, bf16, f32))
        up_in = shift(up, count, 1)
        down_in = shift(down, count, count - 1)
        return blocks, own, (up_in, down_in, far_in)

    def total(own, arrived):
        return own + sum(x.astype(f32) for x in arrived)

    psi_blocks, own, arrived = apply_ham(field, pair_source)
    stack, squares = keep(psi_blocks)
    raw = total(own, arrived)
    denom = jnp.sum(squares)
    rms = jnp.sqrt(denom / (count * size * size))
    first = raw / rms
    blocks, own, arrived = apply_ham(raw.astype(bf16), place_of(pair_source))
    index = jnp.bitwise_xor(jnp.sum(jnp.where((jnp.bitwise_xor(positions, me)[:, None] == positions[None, :]), right_order[None, :], 0), axis=1), me)
    numer = jnp.sum(overlap(index, stack, blocks))
    theta = numer / denom
    second = (total(own, arrived) - theta * raw) / rms
    return first.astype(bf16)[None], second.astype(bf16)[None]


def solution(mesh):
    return jax.shard_map(
        functools.partial(on_device, mesh.shape["op"]),
        mesh=mesh,
        in_specs=(
            P(("groups", "op"), None, None),
            P(("groups", "op"), None, None),
            P(("groups", "op"), None, None),
            P("op"),
            P("op"),
            P("op"),
            P(),
        ),
        out_specs=(P(("groups", "op"), None, None), P(("groups", "op"), None, None)),
        check_vma=False,
    )
```

```python
import functools

import jax
import jax.numpy as jnp
from jax import lax
from jax.experimental import pallas as pl
from jax.experimental.pallas import tpu as pltpu
from jax.sharding import PartitionSpec as P

STRIP = 16
VMEM = pltpu.VMEM
SMEM = pltpu.SMEM
BF16 = jnp.bfloat16
F32 = jnp.float32
STEP = 1 << 32


def in_vmem(x):
    return pltpu.with_memory_space_constraint(x, VMEM)


def in_hbm(x):
    return pltpu.with_memory_space_constraint(x, pltpu.HBM)


def spec(n):
    return [pl.BlockSpec(memory_space=VMEM)] * n


def params(mib):
    return pltpu.CompilerParams(vmem_limit_bytes=mib << 20)


def cost(flops):
    return pl.CostEstimate(flops=flops, bytes_accessed=1, transcendentals=0)


def fold_sum(x):
    return jnp.sum(x.reshape(x.shape[0] // 8, 8, x.shape[1]), axis=0)


def prepare_body(count, me_ref, order, term, source, target, psi, left, right, *refs):
    outs, (psi_out, left_out, right_out) = refs[:8], refs[8:11]
    order_ref, term_ref, source_ref, target_ref, sems = refs[11:]
    copies = [
        pltpu.make_async_copy(a, b, sems.at[i])
        for i, (a, b) in enumerate(
            (
                (order, order_ref),
                (term, term_ref),
                (source, source_ref),
                (target, target_ref),
                (psi, psi_out),
                (left, left_out),
                (right, right_out),
            )
        )
    ]
    for copy in copies:
        copy.start()
    for copy in copies[:4]:
        copy.wait()
    me = me_ref[0]
    terms = left.shape[0]
    place = jnp.zeros(target_ref.shape, jnp.int32)
    source_place = jnp.zeros(source_ref.shape, jnp.int32)
    for j in range(count):
        place = jnp.where(target_ref[...] == order_ref[j], j, place)
        source_place = jnp.where(source_ref[...] == order_ref[j], j, source_place)
    local_term = term_ref[...] - me * terms
    pairs = term_ref.shape[1]
    width = count * STRIP
    columns = lax.broadcasted_iota(jnp.int32, (width, pairs), 0) // STRIP
    rows = lax.broadcasted_iota(jnp.int32, (terms * STRIP, pairs), 0) // STRIP
    owners = (jnp.bitwise_xor(me, count // 2), other_of(me, count), jnp.bitwise_xor(me, 1), me)
    same = (
        lax.broadcasted_iota(jnp.int32, (terms * STRIP, width), 0) % STRIP
        == lax.broadcasted_iota(jnp.int32, (terms * STRIP, width), 1) % STRIP
    )
    for application, sectors in enumerate((source_ref[...], source_place)):
        read = (columns == jnp.bitwise_xor(sectors, me)).astype(F32).astype(BF16)
        for slot, owner in enumerate(owners):
            hit = (rows == local_term) & (place == owner)
            counts = lax.dot_general(
                hit.astype(F32).astype(BF16), read, (((1,), (1,)), ((), ())), preferred_element_type=F32
            )
            outs[application * 4 + slot][...] = jnp.where(same, counts, 0.0).astype(BF16)
    for copy in copies[4:]:
        copy.wait()


def prepare(count, me, order, term, source, target, psi, left_ops, right_ops):
    pairs, terms = term.shape[0], left_ops.shape[0]
    results = pl.pallas_call(
        functools.partial(prepare_body, count),
        out_shape=[pltpu.VMEM((terms * STRIP, count * STRIP), BF16)] * 8
        + [pltpu.VMEM(x.shape, BF16) for x in (psi, left_ops, right_ops)],
        in_specs=[pl.BlockSpec(memory_space=SMEM)] + [pl.BlockSpec(memory_space=pl.ANY)] * 7,
        out_specs=spec(11),
        scratch_shapes=[pltpu.SMEM((count,), jnp.int32)]
        + [pltpu.VMEM((1, pairs), jnp.int32)] * 3
        + [pltpu.SemaphoreType.DMA((7,))],
        cost_estimate=cost(1),
        compiler_params=params(8),
    )(
        me.reshape(1),
        *[in_hbm(x) for x in (order, *[x.reshape(1, pairs) for x in (term, source, target)], psi, left_ops, right_ops)],
    )
    return results[:4], results[4:8], results[8], results[9], results[10]


def products(w_refs, left_ref, right_ref, blocks, outs, mixed, inner):
    terms, size = right_ref.shape[0], right_ref.shape[1]
    slots = len(w_refs)
    weights = jnp.concatenate([w[...] for w in w_refs], axis=0)
    for strip in range(size // STRIP):
        rows = slice(strip * STRIP, (strip + 1) * STRIP)
        stacked = jnp.concatenate([block[rows, :] for block in blocks], axis=0)
        value = jnp.dot(weights, stacked, preferred_element_type=F32)
        mixed[:, :, rows, :] = value.astype(BF16).reshape(slots, terms, STRIP, size)
    for k in range(terms):
        stacked = jnp.concatenate([mixed[t, k] for t in range(slots)], axis=0)
        value = jnp.dot(stacked, right_ref[k], preferred_element_type=F32).astype(BF16)
        for t in range(slots):
            inner[t, k * size : (k + 1) * size, :] = value[t * size : (t + 1) * size]
    for t in range(slots):
        row = jnp.concatenate([left_ref[k] for k in range(terms)], axis=1)
        total = jnp.dot(row, inner[t], preferred_element_type=F32)
        outs[t][...] = total.astype(outs[t].dtype)


def sums_body(count, slots, *refs):
    w_refs, (left_ref, right_ref), refs = refs[:slots], refs[slots : slots + 2], refs[slots + 2 :]
    products(w_refs, left_ref, right_ref, refs[:count], refs[count:-2], *refs[-2:])


def sums(weights, left_ops, right_ops, blocks, types):
    count, slots, (terms, size, _) = len(blocks), len(types), right_ops.shape
    return pl.pallas_call(
        functools.partial(sums_body, count, slots),
        out_shape=[pltpu.VMEM((size, size), t) for t in types],
        in_specs=spec(2 + slots + count),
        out_specs=spec(slots),
        scratch_shapes=[
            pltpu.VMEM((slots, terms, size, size), BF16),
            pltpu.VMEM((slots, terms * size, size), BF16),
        ],
        cost_estimate=cost(1),
        compiler_params=params(12),
    )(*[in_vmem(x) for x in (*weights, left_ops, right_ops, *blocks)])


def small(body, shapes, inputs, flops=1):
    return pl.pallas_call(
        body,
        out_shape=shapes,
        in_specs=spec(len(inputs)),
        out_specs=spec(len(shapes)),
        cost_estimate=cost(flops),
        compiler_params=params(8),
    )(*[in_vmem(x) for x in inputs])


def keep_body(count, *refs):
    blocks, stack, squares = refs[:count], refs[count], refs[count + 1]
    total = jnp.zeros((8, stack.shape[2]), F32)
    for m in range(count):
        value = blocks[m][...]
        stack[m] = value
        wide = value.astype(F32)
        total = total + fold_sum(wide * wide)
    squares[...] = jnp.broadcast_to(jnp.sum(total, keepdims=True), squares.shape)


def overlap_body(count, me_ref, order_ref, stack, *refs):
    blocks, overlap = refs[:count], refs[count]
    me = me_ref[0]
    total = jnp.zeros((8, stack.shape[2]), F32)
    for m in range(count):
        sector = order_ref[jnp.bitwise_xor(me, m)]
        wave = stack[jnp.bitwise_xor(sector, me)].astype(F32)
        total = total + fold_sum(wave * blocks[m][...].astype(F32))
    overlap[...] = jnp.broadcast_to(jnp.sum(total, keepdims=True), overlap.shape)


def overlap_with(me, order, stack, blocks):
    count = len(blocks)
    return pl.pallas_call(
        functools.partial(overlap_body, count),
        out_shape=pltpu.VMEM((8, 128), F32),
        in_specs=[pl.BlockSpec(memory_space=SMEM)] * 2 + spec(1 + count),
        out_specs=spec(1)[0],
        cost_estimate=cost(1),
        compiler_params=params(8),
    )(me.reshape(1), order, in_vmem(stack), *[in_vmem(x) for x in blocks])


def add_body(total, part, out):
    out[...] = total[...] + part[...].astype(F32)


def add(total, part):
    return small(add_body, [pltpu.VMEM(total.shape, F32)], (total, part), STEP)[0]


def raw_body(total, part, raw, sent):
    value = total[...] + part[...].astype(F32)
    raw[...] = value
    sent[...] = value.astype(BF16)


def first_body(count, raw, squares, out):
    rms = jnp.sqrt(squares[:1, :1] / (count * raw.shape[0] * raw.shape[1]))
    out[0] = (raw[...] / rms).astype(BF16)


def second_body(count, total, part, raw, overlap, squares, out):
    rms = jnp.sqrt(squares[:1, :1] / (count * raw.shape[0] * raw.shape[1]))
    theta = overlap[:1, :1] / squares[:1, :1]
    value = total[...] + part[...].astype(F32)
    out[0] = ((value - theta * raw[...]) / rms).astype(BF16)


def other_of(device, count):
    step = jnp.where(device % 2 == 0, count - 1, 1)
    return lax.rem(device + step, count)


def swap(x, count, mask):
    return lax.ppermute(x, "op", [(i, i ^ mask) for i in range(count)])


def swap_other(x, count):
    return lax.ppermute(x, "op", [(i, (i + (1 if i % 2 else count - 1)) % count) for i in range(count)])


def gather_blocks(field, count, prepared=()):
    blocks = {0: field}
    half = count // 2
    for mask in range(2, half, 2):
        blocks[mask] = swap(field, count, mask)
    blocks[half] = swap(field, count, half)
    far = after(blocks[half], *prepared) if prepared else blocks[half]
    for mask in range(2, half, 2):
        blocks[half + mask] = swap(far, count, mask)
    for mask in range(0, count, 2):
        blocks[mask + 1] = swap(blocks[mask], count, 1)
    return [blocks[m] for m in range(count)]


def after(x, *earlier):
    return lax.optimization_barrier((x, *earlier))[0]


def on_device(count, psi, left_ops, right_ops, pair_term, pair_source, pair_target, right_order):
    field = psi[0]
    size = field.shape[0]
    me = lax.axis_index("op").astype(jnp.int32)
    first_w, second_w, psi_block, left, right = prepare(
        count, me, right_order, pair_term, pair_source, pair_target, field, left_ops, right_ops
    )

    def partial_sums(w, blocks):
        (far,) = sums(w[:1], left, right, blocks, (BF16,))
        (other,) = sums((after(w[1], far),), left, right, blocks, (BF16,))
        near, own = sums((after(w[2], other), w[3]), left, right, blocks, (BF16, F32))
        return own, near, (swap(far, count, count // 2), swap_other(other, count), swap(near, count, 1))

    blocks = gather_blocks(field, count, first_w)
    blocks[0] = psi_block
    own, near, (far_in, other_in, near_in) = partial_sums(first_w, blocks)
    blocks[0] = after(blocks[0], near)
    stack, squares = small(
        functools.partial(keep_body, count),
        [pltpu.VMEM((count, size, size), BF16), pltpu.VMEM((8, 128), F32)],
        blocks,
    )
    total = add(add(after(own, squares), far_in), other_in)
    raw, raw_sent = small(
        raw_body, [pltpu.VMEM(own.shape, F32), pltpu.VMEM(own.shape, BF16)], (total, near_in), STEP
    )

    blocks = gather_blocks(raw_sent, count)
    own, near, (far_in, other_in, near_in) = partial_sums(second_w, blocks)
    out_shape = [jax.ShapeDtypeStruct((1, size, size), BF16)]
    (first,) = small(functools.partial(first_body, count), out_shape, (after(raw, near), squares))
    blocks[0] = after(blocks[0], near)
    overlap = overlap_with(me, right_order, stack, blocks)
    own, first = lax.optimization_barrier((own, first))
    total = add(add(after(own, overlap), far_in), other_in)
    (second,) = small(
        functools.partial(second_body, count), out_shape, (total, near_in, raw, overlap, squares), STEP
    )
    return first, second


def solution(mesh):
    return jax.shard_map(
        functools.partial(on_device, mesh.shape["op"]),
        mesh=mesh,
        in_specs=(
            P(("groups", "op"), None, None),
            P(("groups", "op"), None, None),
            P(("groups", "op"), None, None),
            P("op"),
            P("op"),
            P("op"),
            P(),
        ),
        out_specs=(P(("groups", "op"), None, None), P(("groups", "op"), None, None)),
        check_vma=False,
    )
```

```python
import functools

import jax
import jax.numpy as jnp
from jax import lax
from jax.experimental import pallas as pl
from jax.experimental.pallas import tpu as pltpu
from jax.sharding import PartitionSpec as P

STRIP = 16
VMEM = pltpu.VMEM
SMEM = pltpu.SMEM
BF16 = jnp.bfloat16
F32 = jnp.float32
STEP = 1 << 32


def in_vmem(x):
    return pltpu.with_memory_space_constraint(x, VMEM)


def in_hbm(x):
    return pltpu.with_memory_space_constraint(x, pltpu.HBM)


def spec(n):
    return [pl.BlockSpec(memory_space=VMEM)] * n


def params(mib):
    return pltpu.CompilerParams(vmem_limit_bytes=mib << 20)


def cost(flops):
    return pl.CostEstimate(flops=flops, bytes_accessed=1, transcendentals=0)


def fold_sum(x):
    return jnp.sum(x.reshape(x.shape[0] // 8, 8, x.shape[1]), axis=0)


def prepare_body(count, me_ref, order, term, source, target, psi, left, right, *refs):
    outs, (psi_out, left_out, right_out) = refs[:8], refs[8:11]
    order_ref, term_ref, source_ref, target_ref, sems = refs[11:]
    copies = [
        pltpu.make_async_copy(a, b, sems.at[i])
        for i, (a, b) in enumerate(
            (
                (order, order_ref),
                (term, term_ref),
                (source, source_ref),
                (target, target_ref),
                (psi, psi_out),
                (left, left_out),
                (right, right_out),
            )
        )
    ]
    for copy in copies:
        copy.start()
    for copy in copies[:4]:
        copy.wait()
    me = me_ref[0]
    terms = left.shape[0]
    place = jnp.zeros(target_ref.shape, jnp.int32)
    source_place = jnp.zeros(source_ref.shape, jnp.int32)
    for j in range(count):
        place = jnp.where(target_ref[...] == order_ref[j], j, place)
        source_place = jnp.where(source_ref[...] == order_ref[j], j, source_place)
    local_term = term_ref[...] - me * terms
    pairs = term_ref.shape[1]
    width = count * STRIP
    columns = lax.broadcasted_iota(jnp.int32, (width, pairs), 0) // STRIP
    rows = lax.broadcasted_iota(jnp.int32, (terms * STRIP, pairs), 0) // STRIP
    owners = (jnp.bitwise_xor(me, count // 2), other_of(me, count), jnp.bitwise_xor(me, 1), me)
    same = (
        lax.broadcasted_iota(jnp.int32, (terms * STRIP, width), 0) % STRIP
        == lax.broadcasted_iota(jnp.int32, (terms * STRIP, width), 1) % STRIP
    )
    for application, sectors in enumerate((source_ref[...], source_place)):
        read = (columns == jnp.bitwise_xor(sectors, me)).astype(F32).astype(BF16)
        for slot, owner in enumerate(owners):
            hit = (rows == local_term) & (place == owner)
            counts = lax.dot_general(
                hit.astype(F32).astype(BF16), read, (((1,), (1,)), ((), ())), preferred_element_type=F32
            )
            outs[application * 4 + slot][...] = jnp.where(same, counts, 0.0).astype(BF16)
    for copy in copies[4:]:
        copy.wait()


def prepare(count, me, order, term, source, target, psi, left_ops, right_ops):
    pairs, terms = term.shape[0], left_ops.shape[0]
    results = pl.pallas_call(
        functools.partial(prepare_body, count),
        out_shape=[pltpu.VMEM((terms * STRIP, count * STRIP), BF16)] * 8
        + [pltpu.VMEM(x.shape, BF16) for x in (psi, left_ops, right_ops)],
        in_specs=[pl.BlockSpec(memory_space=SMEM)] + [pl.BlockSpec(memory_space=pl.ANY)] * 7,
        out_specs=spec(11),
        scratch_shapes=[pltpu.SMEM((count,), jnp.int32)]
        + [pltpu.VMEM((1, pairs), jnp.int32)] * 3
        + [pltpu.SemaphoreType.DMA((7,))],
        cost_estimate=cost(1),
        compiler_params=params(8),
    )(
        me.reshape(1),
        *[in_hbm(x) for x in (order, *[x.reshape(1, pairs) for x in (term, source, target)], psi, left_ops, right_ops)],
    )
    return results[:4], results[4:8], results[8], results[9], results[10]


def products(w_refs, left_ref, right_ref, blocks, outs, mixed, inner):
    terms, size = right_ref.shape[0], right_ref.shape[1]
    slots = len(w_refs)
    weights = jnp.concatenate([w[...] for w in w_refs], axis=0)
    for strip in range(size // STRIP):
        rows = slice(strip * STRIP, (strip + 1) * STRIP)
        stacked = jnp.concatenate([block[rows, :] for block in blocks], axis=0)
        value = jnp.dot(weights, stacked, preferred_element_type=F32)
        mixed[:, :, rows, :] = value.astype(BF16).reshape(slots, terms, STRIP, size)
    for k in range(terms):
        stacked = jnp.concatenate([mixed[t, k] for t in range(slots)], axis=0)
        value = jnp.dot(stacked, right_ref[k], preferred_element_type=F32).astype(BF16)
        for t in range(slots):
            inner[t, k * size : (k + 1) * size, :] = value[t * size : (t + 1) * size]
    for t in range(slots):
        row = jnp.concatenate([left_ref[k] for k in range(terms)], axis=1)
        total = jnp.dot(row, inner[t], preferred_element_type=F32)
        outs[t][...] = total.astype(outs[t].dtype)


def operand_order(count):
    near = sorted(range(2, count // 2, 2), key=lambda m: -m.bit_count())
    return [m + c for m in (0, *near, *range(count // 2, count, 2)) for c in (0, 1)]


def sums_body(count, slots, *refs):
    w_refs, (left_ref, right_ref), refs = refs[:slots], refs[slots : slots + 2], refs[slots + 2 :]
    order = operand_order(count)
    blocks = [refs[order.index(m)] for m in range(count)]
    products(w_refs, left_ref, right_ref, blocks, refs[count:-2], *refs[-2:])


def sums(weights, left_ops, right_ops, blocks, types):
    count, slots, (terms, size, _) = len(blocks), len(types), right_ops.shape
    return pl.pallas_call(
        functools.partial(sums_body, count, slots),
        out_shape=[pltpu.VMEM((size, size), t) for t in types],
        in_specs=spec(2 + slots + count),
        out_specs=spec(slots),
        scratch_shapes=[
            pltpu.VMEM((slots, terms, size, size), BF16),
            pltpu.VMEM((slots, terms * size, size), BF16),
        ],
        cost_estimate=cost(1),
        compiler_params=params(12),
    )(*[in_vmem(x) for x in (*weights, left_ops, right_ops, *[blocks[m] for m in operand_order(count)])])


def small(body, shapes, inputs, flops=1):
    return pl.pallas_call(
        body,
        out_shape=shapes,
        in_specs=spec(len(inputs)),
        out_specs=spec(len(shapes)),
        cost_estimate=cost(flops),
        compiler_params=params(8),
    )(*[in_vmem(x) for x in inputs])


def keep_body(count, *refs):
    blocks, stack, squares = refs[:count], refs[count], refs[count + 1]
    total = jnp.zeros((8, stack.shape[2]), F32)
    for m in range(count):
        value = blocks[m][...]
        stack[m] = value
        wide = value.astype(F32)
        total = total + fold_sum(wide * wide)
    squares[...] = jnp.broadcast_to(jnp.sum(total, keepdims=True), squares.shape)


def overlap_body(count, me_ref, order_ref, stack, *refs):
    blocks, overlap = refs[:count], refs[count]
    me = me_ref[0]
    total = jnp.zeros((8, stack.shape[2]), F32)
    for m in range(count):
        sector = order_ref[jnp.bitwise_xor(me, m)]
        wave = stack[jnp.bitwise_xor(sector, me)].astype(F32)
        total = total + fold_sum(wave * blocks[m][...].astype(F32))
    overlap[...] = jnp.broadcast_to(jnp.sum(total, keepdims=True), overlap.shape)


def overlap_with(me, order, stack, blocks):
    count = len(blocks)
    return pl.pallas_call(
        functools.partial(overlap_body, count),
        out_shape=pltpu.VMEM((8, 128), F32),
        in_specs=[pl.BlockSpec(memory_space=SMEM)] * 2 + spec(1 + count),
        out_specs=spec(1)[0],
        cost_estimate=cost(1),
        compiler_params=params(8),
    )(me.reshape(1), order, in_vmem(stack), *[in_vmem(x) for x in blocks])


def add_body(total, part, out):
    out[...] = total[...] + part[...].astype(F32)


def add(total, part):
    return small(add_body, [pltpu.VMEM(total.shape, F32)], (total, part), STEP)[0]


def raw_body(total, part, raw, sent):
    value = total[...] + part[...].astype(F32)
    raw[...] = value
    sent[...] = value.astype(BF16)


def first_body(count, raw, squares, out):
    rms = jnp.sqrt(squares[:1, :1] / (count * raw.shape[0] * raw.shape[1]))
    out[0] = (raw[...] / rms).astype(BF16)


def second_body(count, total, part, raw, overlap, squares, out):
    rms = jnp.sqrt(squares[:1, :1] / (count * raw.shape[0] * raw.shape[1]))
    theta = overlap[:1, :1] / squares[:1, :1]
    value = total[...] + part[...].astype(F32)
    out[0] = ((value - theta * raw[...]) / rms).astype(BF16)


def other_of(device, count):
    step = jnp.where(device % 2 == 0, count - 1, 1)
    return lax.rem(device + step, count)


def swap(x, count, mask):
    return lax.ppermute(x, "op", [(i, i ^ mask) for i in range(count)])


def swap_other(x, count):
    return lax.ppermute(x, "op", [(i, (i + (1 if i % 2 else count - 1)) % count) for i in range(count)])


def gather_blocks(field, count, prepared=()):
    blocks = {0: field}
    half = count // 2
    for mask in range(2, half, 2):
        blocks[mask] = swap(field, count, mask)
    blocks[half] = swap(field, count, half)
    for mask in range(2, half, 2):
        far = after(blocks[half], *prepared) if prepared and mask == 2 else blocks[half]
        blocks[half + mask] = swap(far, count, mask)
    for mask in range(0, count, 2):
        blocks[mask + 1] = swap(blocks[mask], count, 1)
    return [blocks[m] for m in range(count)]


def after(x, *earlier):
    return lax.optimization_barrier((x, *earlier))[0]


def on_device(count, psi, left_ops, right_ops, pair_term, pair_source, pair_target, right_order):
    field = psi[0]
    size = field.shape[0]
    me = lax.axis_index("op").astype(jnp.int32)
    first_w, second_w, psi_block, left, right = prepare(
        count, me, right_order, pair_term, pair_source, pair_target, field, left_ops, right_ops
    )

    def partial_sums(w, blocks):
        (far,) = sums(w[:1], left, right, blocks, (BF16,))
        (other,) = sums((after(w[1], far),), left, right, blocks, (BF16,))
        near, own = sums((after(w[2], other), w[3]), left, right, blocks, (BF16, F32))
        return own, near, (swap(far, count, count // 2), swap_other(other, count), swap(near, count, 1))

    blocks = gather_blocks(field, count, first_w)
    blocks[0] = psi_block
    own, near, (far_in, other_in, near_in) = partial_sums(first_w, blocks)
    blocks[0] = after(blocks[0], near)
    stack, squares = small(
        functools.partial(keep_body, count),
        [pltpu.VMEM((count, size, size), BF16), pltpu.VMEM((8, 128), F32)],
        blocks,
    )
    total = add(add(after(own, squares), far_in), other_in)
    raw, raw_sent = small(
        raw_body, [pltpu.VMEM(own.shape, F32), pltpu.VMEM(own.shape, BF16)], (total, near_in), STEP
    )

    blocks = gather_blocks(raw_sent, count)
    own, near, (far_in, other_in, near_in) = partial_sums(second_w, blocks)
    out_shape = [jax.ShapeDtypeStruct((1, size, size), BF16)]
    (first,) = small(functools.partial(first_body, count), out_shape, (after(raw, near), squares))
    blocks[0] = after(blocks[0], near)
    overlap = overlap_with(me, right_order, stack, blocks)
    own, first = lax.optimization_barrier((own, first))
    total = add(add(after(own, overlap), far_in), other_in)
    (second,) = small(
        functools.partial(second_body, count), out_shape, (total, near_in, raw, overlap, squares), STEP
    )
    return first, second


def solution(mesh):
    return jax.shard_map(
        functools.partial(on_device, mesh.shape["op"]),
        mesh=mesh,
        in_specs=(
            P(("groups", "op"), None, None),
            P(("groups", "op"), None, None),
            P(("groups", "op"), None, None),
            P("op"),
            P("op"),
            P("op"),
            P(),
        ),
        out_specs=(P(("groups", "op"), None, None), P(("groups", "op"), None, None)),
        check_vma=False,
    )
```

```python
import functools

import jax
import jax.numpy as jnp
from jax import lax
from jax.experimental import pallas as pl
from jax.experimental.pallas import tpu as pltpu
from jax.sharding import PartitionSpec as P

STRIP = 16
VMEM = pltpu.VMEM
SMEM = pltpu.SMEM
BF16 = jnp.bfloat16
F32 = jnp.float32
STEP = 1 << 32
HOP = 1 << 28


def in_vmem(x):
    return pltpu.with_memory_space_constraint(x, VMEM)


def in_hbm(x):
    return pltpu.with_memory_space_constraint(x, pltpu.HBM)


def spec(n):
    return [pl.BlockSpec(memory_space=VMEM)] * n


def params(mib):
    return pltpu.CompilerParams(vmem_limit_bytes=mib << 20)


def cost(flops):
    return pl.CostEstimate(flops=flops, bytes_accessed=1, transcendentals=0)


def fold_sum(x):
    return jnp.sum(x.reshape(x.shape[0] // 8, 8, x.shape[1]), axis=0)


def prepare_body(count, me_ref, order, term, source, target, psi, left, right, *refs):
    outs, (psi_out, left_out, right_out) = refs[:8], refs[8:11]
    order_ref, term_ref, source_ref, target_ref, sems = refs[11:]
    copies = [
        pltpu.make_async_copy(a, b, sems.at[i])
        for i, (a, b) in enumerate(
            (
                (order, order_ref),
                (term, term_ref),
                (source, source_ref),
                (target, target_ref),
                (psi, psi_out),
                (left, left_out),
                (right, right_out),
            )
        )
    ]
    for copy in copies:
        copy.start()
    for copy in copies[:4]:
        copy.wait()
    me = me_ref[0]
    terms = left.shape[0]
    place = jnp.zeros(target_ref.shape, jnp.int32)
    source_place = jnp.zeros(source_ref.shape, jnp.int32)
    for j in range(count):
        place = jnp.where(target_ref[...] == order_ref[j], j, place)
        source_place = jnp.where(source_ref[...] == order_ref[j], j, source_place)
    local_term = term_ref[...] - me * terms
    pairs = term_ref.shape[1]
    width = count * STRIP
    columns = lax.broadcasted_iota(jnp.int32, (width, pairs), 0) // STRIP
    rows = lax.broadcasted_iota(jnp.int32, (terms * STRIP, pairs), 0) // STRIP
    owners = (jnp.bitwise_xor(me, count // 2), other_of(me, count), jnp.bitwise_xor(me, 1), me)
    same = (
        lax.broadcasted_iota(jnp.int32, (terms * STRIP, width), 0) % STRIP
        == lax.broadcasted_iota(jnp.int32, (terms * STRIP, width), 1) % STRIP
    )
    for application, sectors in enumerate((source_ref[...], source_place)):
        read = (columns == jnp.bitwise_xor(sectors, me)).astype(F32).astype(BF16)
        for slot, owner in enumerate(owners):
            hit = (rows == local_term) & (place == owner)
            counts = lax.dot_general(
                hit.astype(F32).astype(BF16), read, (((1,), (1,)), ((), ())), preferred_element_type=F32
            )
            outs[application * 4 + slot][...] = jnp.where(same, counts, 0.0).astype(BF16)
    for copy in copies[4:]:
        copy.wait()


def prepare(count, me, order, term, source, target, psi, left_ops, right_ops):
    pairs, terms = term.shape[0], left_ops.shape[0]
    results = pl.pallas_call(
        functools.partial(prepare_body, count),
        out_shape=[pltpu.VMEM((terms * STRIP, count * STRIP), BF16)] * 8
        + [pltpu.VMEM(x.shape, BF16) for x in (psi, left_ops, right_ops)],
        in_specs=[pl.BlockSpec(memory_space=SMEM)] + [pl.BlockSpec(memory_space=pl.ANY)] * 7,
        out_specs=spec(11),
        scratch_shapes=[pltpu.SMEM((count,), jnp.int32)]
        + [pltpu.VMEM((1, pairs), jnp.int32)] * 3
        + [pltpu.SemaphoreType.DMA((7,))],
        cost_estimate=cost(1),
        compiler_params=params(8),
    )(
        me.reshape(1),
        *[in_hbm(x) for x in (order, *[x.reshape(1, pairs) for x in (term, source, target)], psi, left_ops, right_ops)],
    )
    return results[:4], results[4:8], results[8], results[9], results[10]


def products(w_refs, left_ref, right_ref, blocks, outs, mixed, inner):
    terms, size = right_ref.shape[0], right_ref.shape[1]
    slots = len(w_refs)
    weights = jnp.concatenate([w[...] for w in w_refs], axis=0)
    for strip in range(size // STRIP):
        rows = slice(strip * STRIP, (strip + 1) * STRIP)
        stacked = jnp.concatenate([block[rows, :] for block in blocks], axis=0)
        value = jnp.dot(weights, stacked, preferred_element_type=F32)
        mixed[:, :, rows, :] = value.astype(BF16).reshape(slots, terms, STRIP, size)
    for k in range(terms):
        stacked = jnp.concatenate([mixed[t, k] for t in range(slots)], axis=0)
        value = jnp.dot(stacked, right_ref[k], preferred_element_type=F32).astype(BF16)
        for t in range(slots):
            inner[t, k * size : (k + 1) * size, :] = value[t * size : (t + 1) * size]
    for t in range(slots):
        row = jnp.concatenate([left_ref[k] for k in range(terms)], axis=1)
        total = jnp.dot(row, inner[t], preferred_element_type=F32)
        outs[t][...] = total.astype(outs[t].dtype)


def operand_order(count):
    near = sorted(range(2, count // 2, 2), key=lambda m: -m.bit_count())
    return [m + c for m in (0, *near, *range(count // 2, count, 2)) for c in (0, 1)]


class Blocks:
    def __init__(self, places, size):
        self.count, self.size = len(places), size
        self.arrays = []
        index = {}
        for m in operand_order(self.count):
            if id(places[m][0]) not in index:
                index[id(places[m][0])] = len(self.arrays)
                self.arrays.append(places[m][0])
        self.places = [(index[id(places[m][0])], places[m][1]) for m in range(self.count)]

    def operands(self):
        return [in_vmem(x) for x in self.arrays]

    def views(self, refs):
        return [refs[i].at[pl.ds(first, self.size)] for i, first in self.places]


def sums_body(blocks, slots, *refs):
    w_refs, (left_ref, right_ref), refs = refs[:slots], refs[slots : slots + 2], refs[slots + 2 :]
    used = len(blocks.arrays)
    products(w_refs, left_ref, right_ref, blocks.views(refs[:used]), refs[used:-2], *refs[-2:])


def sums(weights, left_ops, right_ops, blocks, types):
    slots, (terms, size, _) = len(types), right_ops.shape
    return pl.pallas_call(
        functools.partial(sums_body, blocks, slots),
        out_shape=[pltpu.VMEM((size, size), t) for t in types],
        in_specs=spec(2 + slots + len(blocks.arrays)),
        out_specs=spec(slots),
        scratch_shapes=[
            pltpu.VMEM((slots, terms, size, size), BF16),
            pltpu.VMEM((slots, terms * size, size), BF16),
        ],
        cost_estimate=cost(1),
        compiler_params=params(12),
    )(*[in_vmem(x) for x in (*weights, left_ops, right_ops)], *blocks.operands())


def small(body, shapes, inputs, flops=1):
    return pl.pallas_call(
        body,
        out_shape=shapes,
        in_specs=spec(len(inputs)),
        out_specs=spec(len(shapes)),
        cost_estimate=cost(flops),
        compiler_params=params(8),
    )(*[in_vmem(x) for x in inputs])


def keep_body(blocks, *refs):
    stack, squares = refs[-2:]
    total = jnp.zeros((8, stack.shape[2]), F32)
    for m, block in enumerate(blocks.views(refs)):
        value = block[...]
        stack[m] = value
        wide = value.astype(F32)
        total = total + fold_sum(wide * wide)
    squares[...] = jnp.broadcast_to(jnp.sum(total, keepdims=True), squares.shape)


def overlap_body(blocks, me_ref, order_ref, stack, *refs):
    overlap = refs[-1]
    me = me_ref[0]
    total = jnp.zeros((8, stack.shape[2]), F32)
    for m, block in enumerate(blocks.views(refs)):
        sector = order_ref[jnp.bitwise_xor(me, m)]
        wave = stack[jnp.bitwise_xor(sector, me)].astype(F32)
        total = total + fold_sum(wave * block[...].astype(F32))
    overlap[...] = jnp.broadcast_to(jnp.sum(total, keepdims=True), overlap.shape)


def overlap_with(me, order, stack, blocks):
    return pl.pallas_call(
        functools.partial(overlap_body, blocks),
        out_shape=pltpu.VMEM((8, 128), F32),
        in_specs=[pl.BlockSpec(memory_space=SMEM)] * 2 + spec(1 + len(blocks.arrays)),
        out_specs=spec(1)[0],
        cost_estimate=cost(1),
        compiler_params=params(8),
    )(me.reshape(1), order, in_vmem(stack), *blocks.operands())


def join_body(*refs):
    *parts, out = refs
    first = 0
    for part in parts:
        out[first : first + part.shape[0]] = part[...]
        first += part.shape[0]


def add_body(total, part, out):
    out[...] = total[...] + part[...].astype(F32)


def add(total, part):
    return small(add_body, [pltpu.VMEM(total.shape, F32)], (total, part), STEP)[0]


def raw_body(total, part, raw, sent):
    value = total[...] + part[...].astype(F32)
    raw[...] = value
    sent[...] = value.astype(BF16)


def first_body(count, raw, squares, out):
    rms = jnp.sqrt(squares[:1, :1] / (count * raw.shape[0] * raw.shape[1]))
    out[0] = (raw[...] / rms).astype(BF16)


def second_body(count, total, part, raw, overlap, squares, out):
    rms = jnp.sqrt(squares[:1, :1] / (count * raw.shape[0] * raw.shape[1]))
    theta = overlap[:1, :1] / squares[:1, :1]
    value = total[...] + part[...].astype(F32)
    out[0] = ((value - theta * raw[...]) / rms).astype(BF16)


def other_of(device, count):
    step = jnp.where(device % 2 == 0, count - 1, 1)
    return lax.rem(device + step, count)


def swap(x, count, mask):
    return lax.ppermute(x, "op", [(i, i ^ mask) for i in range(count)])


def swap_other(x, count):
    return lax.ppermute(x, "op", [(i, (i + (1 if i % 2 else count - 1)) % count) for i in range(count)])


def touch(x, flops):
    return pl.pallas_call(
        lambda given, result: None,
        out_shape=pltpu.VMEM(x.shape, x.dtype),
        in_specs=spec(1),
        out_specs=spec(1)[0],
        input_output_aliases={0: 0},
        cost_estimate=cost(flops),
        compiler_params=params(4),
    )(in_vmem(x))


def gather_blocks(field, count, prepared=(), own=None):
    got = {0: field}
    half, size = count // 2, field.shape[0]
    for mask in range(2, half, 2):
        got[mask] = swap(field, count, mask)
    got[half] = touch(swap(field, count, half), HOP)
    for mask in range(2, half, 2):
        far = after(got[half], *prepared) if prepared and mask == 2 else got[half]
        got[half + mask] = swap(far, count, mask)
    got[0] = field if own is None else own
    places = {m: (x, 0) for m, x in got.items()}
    early = [m for m in range(2, half, 2) if m.bit_count() == 1]
    for group in (early, *[[m] for m in range(0, count, 2) if m not in early]):
        part = got[group[0]]
        if len(group) > 1:
            shapes = [pltpu.VMEM((len(group) * size, size), BF16)]
            (part,) = small(join_body, shapes, [got[m] for m in group])
        part = swap(part, count, 1)
        for i, m in enumerate(group):
            places[m + 1] = (part, i * size)
    return Blocks(places, size)


def after(x, *earlier):
    return lax.optimization_barrier((x, *earlier))[0]


def on_device(count, psi, left_ops, right_ops, pair_term, pair_source, pair_target, right_order):
    field = psi[0]
    size = field.shape[0]
    me = lax.axis_index("op").astype(jnp.int32)
    first_w, second_w, psi_block, left, right = prepare(
        count, me, right_order, pair_term, pair_source, pair_target, field, left_ops, right_ops
    )

    def partial_sums(w, blocks):
        (far,) = sums(w[:1], left, right, blocks, (BF16,))
        (other,) = sums((after(w[1], far),), left, right, blocks, (BF16,))
        near, own = sums((after(w[2], other), w[3]), left, right, blocks, (F32, F32))
        return own, near, (swap(far, count, count // 2), swap_other(other, count), swap(near, count, 1))

    blocks = gather_blocks(field, count, first_w, psi_block)
    own, near, (far_in, other_in, near_in) = partial_sums(first_w, blocks)
    blocks.arrays[0] = after(blocks.arrays[0], near)
    stack, squares = small(
        functools.partial(keep_body, blocks),
        [pltpu.VMEM((count, size, size), BF16), pltpu.VMEM((8, 128), F32)],
        blocks.arrays,
    )
    total = add(add(after(own, squares), far_in), other_in)
    raw, raw_sent = small(
        raw_body, [pltpu.VMEM(own.shape, F32), pltpu.VMEM(own.shape, BF16)], (total, near_in), STEP
    )

    blocks = gather_blocks(raw_sent, count)
    own, near, (far_in, other_in, near_in) = partial_sums(second_w, blocks)
    out_shape = [jax.ShapeDtypeStruct((1, size, size), BF16)]
    (first,) = small(functools.partial(first_body, count), out_shape, (after(raw, near), squares))
    blocks.arrays[0] = after(blocks.arrays[0], near)
    overlap = overlap_with(me, right_order, stack, blocks)
    own, first = lax.optimization_barrier((own, first))
    total = add(add(after(own, overlap), far_in), other_in)
    (second,) = small(
        functools.partial(second_body, count), out_shape, (total, near_in, raw, overlap, squares), STEP
    )
    return first, second


def solution(mesh):
    return jax.shard_map(
        functools.partial(on_device, mesh.shape["op"]),
        mesh=mesh,
        in_specs=(
            P(("groups", "op"), None, None),
            P(("groups", "op"), None, None),
            P(("groups", "op"), None, None),
            P("op"),
            P("op"),
            P("op"),
            P(),
        ),
        out_specs=(P(("groups", "op"), None, None), P(("groups", "op"), None, None)),
        check_vma=False,
    )
```

```python
import functools

import jax
import jax.numpy as jnp
from jax import lax
from jax.experimental import pallas as pl
from jax.experimental.pallas import tpu as pltpu
from jax.sharding import PartitionSpec as P

STRIP = 16
VMEM = pltpu.VMEM
SMEM = pltpu.SMEM
BF16 = jnp.bfloat16
F32 = jnp.float32
STEP = 1 << 32
HOP = 1 << 28


def in_vmem(x):
    return pltpu.with_memory_space_constraint(x, VMEM)


def in_hbm(x):
    return pltpu.with_memory_space_constraint(x, pltpu.HBM)


def spec(n):
    return [pl.BlockSpec(memory_space=VMEM)] * n


def params(mib):
    return pltpu.CompilerParams(vmem_limit_bytes=mib << 20)


def cost(flops):
    return pl.CostEstimate(flops=flops, bytes_accessed=1, transcendentals=0)


def fold_sum(x):
    return jnp.sum(x.reshape(x.shape[0] // 8, 8, x.shape[1]), axis=0)


def prepare_body(count, me_ref, order, term, source, target, psi, left, right, *refs):
    outs, (psi_out, left_out, right_out) = refs[:8], refs[8:11]
    order_ref, term_ref, source_ref, target_ref, sems = refs[11:]
    copies = [
        pltpu.make_async_copy(a, b, sems.at[i])
        for i, (a, b) in enumerate(
            (
                (order, order_ref),
                (term, term_ref),
                (source, source_ref),
                (target, target_ref),
                (psi, psi_out),
                (left, left_out),
                (right, right_out),
            )
        )
    ]
    for copy in copies:
        copy.start()
    for copy in copies[:4]:
        copy.wait()
    me = me_ref[0]
    terms = left.shape[0]
    place = jnp.zeros(target_ref.shape, jnp.int32)
    source_place = jnp.zeros(source_ref.shape, jnp.int32)
    for j in range(count):
        place = jnp.where(target_ref[...] == order_ref[j], j, place)
        source_place = jnp.where(source_ref[...] == order_ref[j], j, source_place)
    local_term = term_ref[...] - me * terms
    pairs = term_ref.shape[1]
    width = count * STRIP
    columns = lax.broadcasted_iota(jnp.int32, (width, pairs), 0) // STRIP
    rows = lax.broadcasted_iota(jnp.int32, (terms * STRIP, pairs), 0) // STRIP
    owners = (jnp.bitwise_xor(me, count // 2), other_of(me, count), jnp.bitwise_xor(me, 1), me)
    same = (
        lax.broadcasted_iota(jnp.int32, (terms * STRIP, width), 0) % STRIP
        == lax.broadcasted_iota(jnp.int32, (terms * STRIP, width), 1) % STRIP
    )
    for application, sectors in enumerate((source_ref[...], source_place)):
        read = (columns == jnp.bitwise_xor(sectors, me)).astype(F32).astype(BF16)
        for slot, owner in enumerate(owners):
            hit = (rows == local_term) & (place == owner)
            counts = lax.dot_general(
                hit.astype(F32).astype(BF16), read, (((1,), (1,)), ((), ())), preferred_element_type=F32
            )
            outs[application * 4 + slot][...] = jnp.where(same, counts, 0.0).astype(BF16)
    for copy in copies[4:]:
        copy.wait()


def prepare(count, me, order, term, source, target, psi, left_ops, right_ops):
    pairs, terms = term.shape[0], left_ops.shape[0]
    results = pl.pallas_call(
        functools.partial(prepare_body, count),
        out_shape=[pltpu.VMEM((terms * STRIP, count * STRIP), BF16)] * 8
        + [pltpu.VMEM(x.shape, BF16) for x in (psi, left_ops, right_ops)],
        in_specs=[pl.BlockSpec(memory_space=SMEM)] + [pl.BlockSpec(memory_space=pl.ANY)] * 7,
        out_specs=spec(11),
        scratch_shapes=[pltpu.SMEM((count,), jnp.int32)]
        + [pltpu.VMEM((1, pairs), jnp.int32)] * 3
        + [pltpu.SemaphoreType.DMA((7,))],
        cost_estimate=cost(1),
        compiler_params=params(8),
    )(
        me.reshape(1),
        *[in_hbm(x) for x in (order, *[x.reshape(1, pairs) for x in (term, source, target)], psi, left_ops, right_ops)],
    )
    return results[:4], results[4:8], results[8], results[9], results[10]


def products(w_refs, left_ref, right_ref, blocks, outs, mixed, inner):
    terms, size = right_ref.shape[0], right_ref.shape[1]
    slots = len(w_refs)
    weights = jnp.concatenate([w[...] for w in w_refs], axis=0)
    for strip in range(size // STRIP):
        rows = slice(strip * STRIP, (strip + 1) * STRIP)
        stacked = jnp.concatenate([block[rows, :] for block in blocks], axis=0)
        value = jnp.dot(weights, stacked, preferred_element_type=F32)
        mixed[:, :, rows, :] = value.astype(BF16).reshape(slots, terms, STRIP, size)
    for k in range(terms):
        stacked = jnp.concatenate([mixed[t, k] for t in range(slots)], axis=0)
        value = jnp.dot(stacked, right_ref[k], preferred_element_type=F32).astype(BF16)
        for t in range(slots):
            inner[t, k * size : (k + 1) * size, :] = value[t * size : (t + 1) * size]
    for t in range(slots):
        for rows in (slice(0, size // 2), slice(size // 2, size)):
            row = jnp.concatenate([left_ref[k, rows, :] for k in range(terms)], axis=1)
            total = jnp.dot(row, inner[t], preferred_element_type=F32)
            outs[t][rows, :] = total.astype(outs[t].dtype)


def operand_order(count):
    near = sorted(range(2, count // 2, 2), key=lambda m: -m.bit_count())
    return [m + c for m in (0, *near, *range(count // 2, count, 2)) for c in (0, 1)]


class Blocks:
    def __init__(self, places, size):
        self.count, self.size = len(places), size
        self.arrays = []
        index = {}
        for m in operand_order(self.count):
            if id(places[m][0]) not in index:
                index[id(places[m][0])] = len(self.arrays)
                self.arrays.append(places[m][0])
        self.places = [(index[id(places[m][0])], places[m][1]) for m in range(self.count)]

    def operands(self):
        return [in_vmem(x) for x in self.arrays]

    def views(self, refs):
        return [refs[i].at[pl.ds(first, self.size)] for i, first in self.places]


def sums_body(blocks, slots, *refs):
    w_refs, (left_ref, right_ref), refs = refs[:slots], refs[slots : slots + 2], refs[slots + 2 :]
    used = len(blocks.arrays)
    products(w_refs, left_ref, right_ref, blocks.views(refs[:used]), refs[used:-2], *refs[-2:])


def sums(weights, left_ops, right_ops, blocks, types):
    slots, (terms, size, _) = len(types), right_ops.shape
    return pl.pallas_call(
        functools.partial(sums_body, blocks, slots),
        out_shape=[pltpu.VMEM((size, size), t) for t in types],
        in_specs=spec(2 + slots + len(blocks.arrays)),
        out_specs=spec(slots),
        scratch_shapes=[
            pltpu.VMEM((slots, terms, size, size), BF16),
            pltpu.VMEM((slots, terms * size, size), BF16),
        ],
        cost_estimate=cost(1),
        compiler_params=params(12),
    )(*[in_vmem(x) for x in (*weights, left_ops, right_ops)], *blocks.operands())


def small(body, shapes, inputs, flops=1):
    return pl.pallas_call(
        body,
        out_shape=shapes,
        in_specs=spec(len(inputs)),
        out_specs=spec(len(shapes)),
        cost_estimate=cost(flops),
        compiler_params=params(8),
    )(*[in_vmem(x) for x in inputs])


def keep_body(blocks, *refs):
    stack, squares = refs[-2:]
    total = jnp.zeros((8, stack.shape[2]), F32)
    for m, block in enumerate(blocks.views(refs)):
        value = block[...]
        stack[m] = value
        wide = value.astype(F32)
        total = total + fold_sum(wide * wide)
    squares[...] = jnp.broadcast_to(jnp.sum(total, keepdims=True), squares.shape)


def overlap_body(blocks, me_ref, order_ref, stack, *refs):
    overlap = refs[-1]
    me = me_ref[0]
    total = jnp.zeros((8, stack.shape[2]), F32)
    for m, block in enumerate(blocks.views(refs)):
        sector = order_ref[jnp.bitwise_xor(me, m)]
        wave = stack[jnp.bitwise_xor(sector, me)].astype(F32)
        total = total + fold_sum(wave * block[...].astype(F32))
    overlap[...] = jnp.broadcast_to(jnp.sum(total, keepdims=True), overlap.shape)


def overlap_with(me, order, stack, blocks):
    return pl.pallas_call(
        functools.partial(overlap_body, blocks),
        out_shape=pltpu.VMEM((8, 128), F32),
        in_specs=[pl.BlockSpec(memory_space=SMEM)] * 2 + spec(1 + len(blocks.arrays)),
        out_specs=spec(1)[0],
        cost_estimate=cost(1),
        compiler_params=params(8),
    )(me.reshape(1), order, in_vmem(stack), *blocks.operands())


def join_body(*refs):
    *parts, out = refs
    first = 0
    for part in parts:
        out[first : first + part.shape[0]] = part[...]
        first += part.shape[0]


def add_body(total, part, out):
    out[...] = total[...] + part[...].astype(F32)


def add(total, part):
    return small(add_body, [pltpu.VMEM(total.shape, F32)], (total, part), STEP)[0]


def raw_body(total, part, raw, sent):
    value = total[...] + part[...].astype(F32)
    raw[...] = value
    sent[...] = value.astype(BF16)


def first_body(count, raw, squares, out):
    rms = jnp.sqrt(squares[:1, :1] / (count * raw.shape[0] * raw.shape[1]))
    out[0] = (raw[...] / rms).astype(BF16)


def second_body(count, total, part, raw, overlap, squares, out):
    rms = jnp.sqrt(squares[:1, :1] / (count * raw.shape[0] * raw.shape[1]))
    theta = overlap[:1, :1] / squares[:1, :1]
    value = total[...] + part[...].astype(F32)
    out[0] = ((value - theta * raw[...]) / rms).astype(BF16)


def other_of(device, count):
    step = jnp.where(device % 2 == 0, count - 1, 1)
    return lax.rem(device + step, count)


def swap(x, count, mask):
    return lax.ppermute(x, "op", [(i, i ^ mask) for i in range(count)])


def swap_other(x, count):
    return lax.ppermute(x, "op", [(i, (i + (1 if i % 2 else count - 1)) % count) for i in range(count)])


def touch(x, flops):
    return pl.pallas_call(
        lambda given, result: None,
        out_shape=pltpu.VMEM(x.shape, x.dtype),
        in_specs=spec(1),
        out_specs=spec(1)[0],
        input_output_aliases={0: 0},
        cost_estimate=cost(flops),
        compiler_params=params(4),
    )(in_vmem(x))


def gather_blocks(field, count, prepared=(), own=None):
    got = {0: field}
    half, size = count // 2, field.shape[0]
    for mask in range(2, half, 2):
        got[mask] = swap(field, count, mask)
    got[half] = touch(swap(field, count, half), HOP)
    for mask in range(2, half, 2):
        far = after(got[half], *prepared) if prepared and mask == 2 else got[half]
        got[half + mask] = swap(far, count, mask)
    got[0] = field if own is None else own
    places = {m: (x, 0) for m, x in got.items()}
    early = [m for m in range(2, half, 2) if m.bit_count() == 1]
    for group in (early, *[[m] for m in range(0, count, 2) if m not in early]):
        part = got[group[0]]
        if len(group) > 1:
            shapes = [pltpu.VMEM((len(group) * size, size), BF16)]
            (part,) = small(join_body, shapes, [got[m] for m in group])
        part = swap(part, count, 1)
        for i, m in enumerate(group):
            places[m + 1] = (part, i * size)
    return Blocks(places, size)


def after(x, *earlier):
    return lax.optimization_barrier((x, *earlier))[0]


def on_device(count, psi, left_ops, right_ops, pair_term, pair_source, pair_target, right_order):
    field = psi[0]
    size = field.shape[0]
    me = lax.axis_index("op").astype(jnp.int32)
    first_w, second_w, psi_block, left, right = prepare(
        count, me, right_order, pair_term, pair_source, pair_target, field, left_ops, right_ops
    )

    def partial_sums(w, blocks):
        (far,) = sums(w[:1], left, right, blocks, (BF16,))
        (other,) = sums((after(w[1], far),), left, right, blocks, (BF16,))
        near, own = sums((after(w[2], other), w[3]), left, right, blocks, (F32, F32))
        return own, near, (swap(far, count, count // 2), swap_other(other, count), swap(near, count, 1))

    blocks = gather_blocks(field, count, first_w, psi_block)
    own, near, (far_in, other_in, near_in) = partial_sums(first_w, blocks)
    blocks.arrays[0] = after(blocks.arrays[0], near)
    stack, squares = small(
        functools.partial(keep_body, blocks),
        [pltpu.VMEM((count, size, size), BF16), pltpu.VMEM((8, 128), F32)],
        blocks.arrays,
    )
    total = add(add(after(own, squares), far_in), other_in)
    raw, raw_sent = small(
        raw_body, [pltpu.VMEM(own.shape, F32), pltpu.VMEM(own.shape, BF16)], (total, near_in), STEP
    )

    blocks = gather_blocks(raw_sent, count)
    own, near, (far_in, other_in, near_in) = partial_sums(second_w, blocks)
    out_shape = [jax.ShapeDtypeStruct((1, size, size), BF16)]
    (first,) = small(functools.partial(first_body, count), out_shape, (after(raw, near), squares))
    blocks.arrays[0] = after(blocks.arrays[0], near)
    overlap = overlap_with(me, right_order, stack, blocks)
    own, first = lax.optimization_barrier((own, first))
    total = add(add(after(own, overlap), far_in), other_in)
    (second,) = small(
        functools.partial(second_body, count), out_shape, (total, near_in, raw, overlap, squares), STEP
    )
    return first, second


def solution(mesh):
    return jax.shard_map(
        functools.partial(on_device, mesh.shape["op"]),
        mesh=mesh,
        in_specs=(
            P(("groups", "op"), None, None),
            P(("groups", "op"), None, None),
            P(("groups", "op"), None, None),
            P("op"),
            P("op"),
            P("op"),
            P(),
        ),
        out_specs=(P(("groups", "op"), None, None), P(("groups", "op"), None, None)),
        check_vma=False,
    )
```

```python
import functools

import jax
import jax.numpy as jnp
from jax import lax
from jax.experimental import pallas as pl
from jax.experimental.pallas import tpu as pltpu
from jax.sharding import PartitionSpec as P

STRIP = 16
VMEM = pltpu.VMEM
SMEM = pltpu.SMEM
BF16 = jnp.bfloat16
F32 = jnp.float32
STEP = 1 << 32
HOP = 1 << 28


def in_vmem(x):
    return pltpu.with_memory_space_constraint(x, VMEM)


def in_hbm(x):
    return pltpu.with_memory_space_constraint(x, pltpu.HBM)


def spec(n):
    return [pl.BlockSpec(memory_space=VMEM)] * n


def params(mib):
    return pltpu.CompilerParams(vmem_limit_bytes=mib << 20)


def cost(flops):
    return pl.CostEstimate(flops=flops, bytes_accessed=1, transcendentals=0)


def fold_sum(x):
    return jnp.sum(x.reshape(x.shape[0] // 8, 8, x.shape[1]), axis=0)


def prepare_body(count, me_ref, order, term, source, target, psi, left, right, *refs):
    outs, (psi_out, left_out, right_out) = refs[:8], refs[8:11]
    order_ref, term_ref, source_ref, target_ref, sems = refs[11:]
    copies = [
        pltpu.make_async_copy(a, b, sems.at[i])
        for i, (a, b) in enumerate(
            (
                (order, order_ref),
                (term, term_ref),
                (source, source_ref),
                (target, target_ref),
                (psi, psi_out),
                (left, left_out),
                (right, right_out),
            )
        )
    ]
    for copy in copies:
        copy.start()
    for copy in copies[:4]:
        copy.wait()
    me = me_ref[0]
    terms = left.shape[0]
    place = jnp.zeros(target_ref.shape, jnp.int32)
    source_place = jnp.zeros(source_ref.shape, jnp.int32)
    for j in range(count):
        place = jnp.where(target_ref[...] == order_ref[j], j, place)
        source_place = jnp.where(source_ref[...] == order_ref[j], j, source_place)
    local_term = term_ref[...] - me * terms
    pairs = term_ref.shape[1]
    width = count * STRIP
    columns = lax.broadcasted_iota(jnp.int32, (width, pairs), 0) // STRIP
    rows = lax.broadcasted_iota(jnp.int32, (terms * STRIP, pairs), 0) // STRIP
    owners = (jnp.bitwise_xor(me, count // 2), other_of(me, count), jnp.bitwise_xor(me, 1), me)
    same = (
        lax.broadcasted_iota(jnp.int32, (terms * STRIP, width), 0) % STRIP
        == lax.broadcasted_iota(jnp.int32, (terms * STRIP, width), 1) % STRIP
    )
    for application, sectors in enumerate((source_ref[...], source_place)):
        read = (columns == jnp.bitwise_xor(sectors, me)).astype(F32).astype(BF16)
        for slot, owner in enumerate(owners):
            hit = (rows == local_term) & (place == owner)
            counts = lax.dot_general(
                hit.astype(F32).astype(BF16), read, (((1,), (1,)), ((), ())), preferred_element_type=F32
            )
            outs[application * 4 + slot][...] = jnp.where(same, counts, 0.0).astype(BF16)
    for copy in copies[4:]:
        copy.wait()


def prepare(count, me, order, term, source, target, psi, left_ops, right_ops):
    pairs, terms = term.shape[0], left_ops.shape[0]
    results = pl.pallas_call(
        functools.partial(prepare_body, count),
        out_shape=[pltpu.VMEM((terms * STRIP, count * STRIP), BF16)] * 8
        + [pltpu.VMEM(x.shape, BF16) for x in (psi, left_ops, right_ops)],
        in_specs=[pl.BlockSpec(memory_space=SMEM)] + [pl.BlockSpec(memory_space=pl.ANY)] * 7,
        out_specs=spec(11),
        scratch_shapes=[pltpu.SMEM((count,), jnp.int32)]
        + [pltpu.VMEM((1, pairs), jnp.int32)] * 3
        + [pltpu.SemaphoreType.DMA((7,))],
        cost_estimate=cost(1),
        compiler_params=params(8),
    )(
        me.reshape(1),
        *[in_hbm(x) for x in (order, *[x.reshape(1, pairs) for x in (term, source, target)], psi, left_ops, right_ops)],
    )
    return results[:4], results[4:8], results[8], results[9], results[10]


def products(w_refs, left_ref, right_ref, blocks, outs, mixed, inner):
    terms, size = right_ref.shape[0], right_ref.shape[1]
    slots = len(w_refs)
    weights = jnp.concatenate([w[...] for w in w_refs], axis=0)
    for strip in range(size // STRIP):
        rows = slice(strip * STRIP, (strip + 1) * STRIP)
        stacked = jnp.concatenate([block[rows, :] for block in blocks], axis=0)
        value = jnp.dot(weights, stacked, preferred_element_type=F32)
        mixed[:, :, rows, :] = value.astype(BF16).reshape(slots, terms, STRIP, size)
    for k in range(terms):
        stacked = jnp.concatenate([mixed[t, k] for t in range(slots)], axis=0)
        value = jnp.dot(stacked, right_ref[k], preferred_element_type=F32).astype(BF16)
        for t in range(slots):
            inner[t, k * size : (k + 1) * size, :] = value[t * size : (t + 1) * size]
    for t in range(slots):
        for rows in (slice(0, size // 2), slice(size // 2, size)):
            row = jnp.concatenate([left_ref[k, rows, :] for k in range(terms)], axis=1)
            total = jnp.dot(row, inner[t], preferred_element_type=F32)
            outs[t][rows, :] = total.astype(outs[t].dtype)


def operand_order(count):
    near = sorted(range(2, count // 2, 2), key=lambda m: -m.bit_count())
    return [m + c for m in (0, *near, *range(count // 2, count, 2)) for c in (0, 1)]


class Blocks:
    def __init__(self, places, size):
        self.count, self.size = len(places), size
        self.arrays = []
        index = {}
        for m in operand_order(self.count):
            if id(places[m][0]) not in index:
                index[id(places[m][0])] = len(self.arrays)
                self.arrays.append(places[m][0])
        self.places = [(index[id(places[m][0])], places[m][1]) for m in range(self.count)]

    def operands(self):
        return [in_vmem(x) for x in self.arrays]

    def views(self, refs):
        return [refs[i].at[pl.ds(first, self.size)] for i, first in self.places]


def sums_body(blocks, slots, *refs):
    w_refs, (left_ref, right_ref), refs = refs[:slots], refs[slots : slots + 2], refs[slots + 2 :]
    used = len(blocks.arrays)
    products(w_refs, left_ref, right_ref, blocks.views(refs[:used]), refs[used:-2], *refs[-2:])


def sums(weights, left_ops, right_ops, blocks, types):
    slots, (terms, size, _) = len(types), right_ops.shape
    return pl.pallas_call(
        functools.partial(sums_body, blocks, slots),
        out_shape=[pltpu.VMEM((size, size), t) for t in types],
        in_specs=spec(2 + slots + len(blocks.arrays)),
        out_specs=spec(slots),
        scratch_shapes=[
            pltpu.VMEM((slots, terms, size, size), BF16),
            pltpu.VMEM((slots, terms * size, size), BF16),
        ],
        cost_estimate=cost(1),
        compiler_params=params(12),
    )(*[in_vmem(x) for x in (*weights, left_ops, right_ops)], *blocks.operands())


def small(body, shapes, inputs, flops=1):
    return pl.pallas_call(
        body,
        out_shape=shapes,
        in_specs=spec(len(inputs)),
        out_specs=spec(len(shapes)),
        cost_estimate=cost(flops),
        compiler_params=params(8),
    )(*[in_vmem(x) for x in inputs])


def keep_body(blocks, *refs):
    stack, squares = refs[-2:]
    total = jnp.zeros((8, stack.shape[2]), F32)
    for m, block in enumerate(blocks.views(refs)):
        value = block[...]
        stack[m] = value
        wide = value.astype(F32)
        total = total + fold_sum(wide * wide)
    squares[...] = jnp.broadcast_to(jnp.sum(total, keepdims=True), squares.shape)


def overlap_body(blocks, me_ref, order_ref, stack, *refs):
    overlap = refs[-1]
    me = me_ref[0]
    total = jnp.zeros((8, stack.shape[2]), F32)
    for m, block in enumerate(blocks.views(refs)):
        sector = order_ref[jnp.bitwise_xor(me, m)]
        wave = stack[jnp.bitwise_xor(sector, me)].astype(F32)
        total = total + fold_sum(wave * block[...].astype(F32))
    overlap[...] = jnp.broadcast_to(jnp.sum(total, keepdims=True), overlap.shape)


def overlap_with(me, order, stack, blocks):
    return pl.pallas_call(
        functools.partial(overlap_body, blocks),
        out_shape=pltpu.VMEM((8, 128), F32),
        in_specs=[pl.BlockSpec(memory_space=SMEM)] * 2 + spec(1 + len(blocks.arrays)),
        out_specs=spec(1)[0],
        cost_estimate=cost(1),
        compiler_params=params(8),
    )(me.reshape(1), order, in_vmem(stack), *blocks.operands())


def join_body(*refs):
    *parts, out = refs
    first = 0
    for part in parts:
        out[first : first + part.shape[0]] = part[...]
        first += part.shape[0]


def add_body(total, part, out):
    out[...] = total[...] + part[...].astype(F32)


def add(total, part):
    return small(add_body, [pltpu.VMEM(total.shape, F32)], (total, part), STEP)[0]


def raw_body(total, part, raw, sent):
    value = total[...] + part[...].astype(F32)
    raw[...] = value
    sent[...] = value.astype(BF16)


def first_body(count, raw, squares, out):
    rms = jnp.sqrt(squares[:1, :1] / (count * raw.shape[0] * raw.shape[1]))
    out[0] = (raw[...] / rms).astype(BF16)


def second_body(count, total, part, raw, overlap, squares, out):
    rms = jnp.sqrt(squares[:1, :1] / (count * raw.shape[0] * raw.shape[1]))
    theta = overlap[:1, :1] / squares[:1, :1]
    value = total[...] + part[...].astype(F32)
    out[0] = ((value - theta * raw[...]) / rms).astype(BF16)


def other_of(device, count):
    step = jnp.where(device % 2 == 0, count - 1, 1)
    return lax.rem(device + step, count)


def swap(x, count, mask):
    return lax.ppermute(x, "op", [(i, i ^ mask) for i in range(count)])


def swap_other(x, count):
    return lax.ppermute(x, "op", [(i, (i + (1 if i % 2 else count - 1)) % count) for i in range(count)])


def touch(x, flops):
    return pl.pallas_call(
        lambda given, result: None,
        out_shape=pltpu.VMEM(x.shape, x.dtype),
        in_specs=spec(1),
        out_specs=spec(1)[0],
        input_output_aliases={0: 0},
        cost_estimate=cost(flops),
        compiler_params=params(4),
    )(in_vmem(x))


def gather_blocks(field, count, prepared=(), own=None):
    got = {0: field}
    half, size = count // 2, field.shape[0]
    for mask in range(2, half, 2):
        got[mask] = swap(field, count, mask)
    got[half] = touch(swap(field, count, half), HOP)
    for mask in range(2, half, 2):
        got[half + mask] = swap(got[half], count, mask)
    got[0] = field if own is None else own
    places = {m: (x, 0) for m, x in got.items()}
    near = range(2, half, 2)
    early, late = ([m for m in near if (m.bit_count() == 1) == single] for single in (True, False))
    for group in (early, [0], [half, *late], *[[half + m] for m in near]):
        part = got[group[0]]
        if prepared and group == [0]:
            part = after(part, *prepared)
        if len(group) > 1:
            shapes = [pltpu.VMEM((len(group) * size, size), BF16)]
            (part,) = small(join_body, shapes, [got[m] for m in group])
        part = swap(part, count, 1)
        for i, m in enumerate(group):
            places[m + 1] = (part, i * size)
    return Blocks(places, size)


def after(x, *earlier):
    return lax.optimization_barrier((x, *earlier))[0]


def on_device(count, psi, left_ops, right_ops, pair_term, pair_source, pair_target, right_order):
    field = psi[0]
    size = field.shape[0]
    me = lax.axis_index("op").astype(jnp.int32)
    first_w, second_w, psi_block, left, right = prepare(
        count, me, right_order, pair_term, pair_source, pair_target, field, left_ops, right_ops
    )

    def partial_sums(w, blocks):
        (far,) = sums(w[:1], left, right, blocks, (BF16,))
        (other,) = sums((after(w[1], far),), left, right, blocks, (BF16,))
        near, own = sums((after(w[2], other), w[3]), left, right, blocks, (F32, F32))
        return own, near, (swap(far, count, count // 2), swap_other(other, count), swap(near, count, 1))

    blocks = gather_blocks(field, count, first_w, psi_block)
    own, near, (far_in, other_in, near_in) = partial_sums(first_w, blocks)
    blocks.arrays[0] = after(blocks.arrays[0], near)
    stack, squares = small(
        functools.partial(keep_body, blocks),
        [pltpu.VMEM((count, size, size), BF16), pltpu.VMEM((8, 128), F32)],
        blocks.arrays,
    )
    total = add(add(after(own, squares), far_in), other_in)
    raw, raw_sent = small(
        raw_body, [pltpu.VMEM(own.shape, F32), pltpu.VMEM(own.shape, BF16)], (total, near_in), STEP
    )

    blocks = gather_blocks(raw_sent, count)
    own, near, (far_in, other_in, near_in) = partial_sums(second_w, blocks)
    out_shape = [jax.ShapeDtypeStruct((1, size, size), BF16)]
    (first,) = small(functools.partial(first_body, count), out_shape, (after(raw, near), squares))
    blocks.arrays[0] = after(blocks.arrays[0], near)
    overlap = overlap_with(me, right_order, stack, blocks)
    own, first = lax.optimization_barrier((own, first))
    total = add(add(after(own, overlap), far_in), other_in)
    (second,) = small(
        functools.partial(second_body, count), out_shape, (total, near_in, raw, overlap, squares), STEP
    )
    return first, second


def solution(mesh):
    return jax.shard_map(
        functools.partial(on_device, mesh.shape["op"]),
        mesh=mesh,
        in_specs=(
            P(("groups", "op"), None, None),
            P(("groups", "op"), None, None),
            P(("groups", "op"), None, None),
            P("op"),
            P("op"),
            P("op"),
            P(),
        ),
        out_specs=(P(("groups", "op"), None, None), P(("groups", "op"), None, None)),
        check_vma=False,
    )
```
